32 devices in a mesh: dp: 2 (over y), seq: 4 (over z), tensor: 4 (over x, core).
Axes of the slice: x: 2, y: 2, z: 4, core: 2. Of those that a mesh axis runs over, the one named last changes fastest.
Arguments:
- tokens: bfloat16 [8, 1500, 768], P(('dp', 'tensor'), 'seq'), may hold values from -6 to 6
- ln1_gain: bfloat16 [768], replicated, may hold values from 0.5 to 1.5
- ln1_bias: bfloat16 [768], replicated, may hold values from -3 to 3
- w_qkv: bfloat16 [3, 768, 768], P(None, None, 'tensor'), may hold values from -0.21875 to 0.21875
- b_query_value: bfloat16 [2, 768], P(None, 'tensor'), may hold values from -3 to 3
- w_out: bfloat16 [768, 768], P('tensor'), may hold values from -4 to 4
- b_out: bfloat16 [768], replicated, may hold values from -3 to 3
- ln2_gain: bfloat16 [768], replicated, may hold values from 0.5 to 1.5
- ln2_bias: bfloat16 [768], replicated, may hold values from -3 to 3
- w_up: bfloat16 [768, 3072], P(None, 'tensor'), may hold values from -0.21875 to 0.21875
- b_up: bfloat16 [3072], P('tensor'), may hold values from -3 to 3
- w_down: bfloat16 [3072, 768], P('tensor'), may hold values from -0.109375 to 0.109375
- b_down: bfloat16 [768], replicated, may hold values from -3 to 3
- cotangent: bfloat16 [8, 1500, 768], P(('dp', 'tensor'), 'seq'), may hold values from -6 to 6
Outputs:
- output: bfloat16 [8, 1500, 768], P(('dp', 'tensor'), 'seq')
- grad_tokens: bfloat16 [8, 1500, 768], P(('dp', 'tensor'), 'seq')
- grad_ln1_gain: float32 [768], P('tensor')
- grad_ln1_bias: float32 [768], P('tensor')
- grad_qkv: float32 [3, 768, 768], P(None, None, 'tensor')
- grad_qv_bias: float32 [2, 768], P(None, 'tensor')
- grad_out: float32 [768, 768], P('tensor')
- grad_out_bias: float32 [768], P('tensor')
- grad_ln2_gain: float32 [768], P('tensor')
- grad_ln2_bias: float32 [768], P('tensor')
- grad_up: float32 [768, 3072], P(None, 'tensor')
- grad_up_bias: float32 [3072], P('tensor')
- grad_down: float32 [3072, 768], P('tensor')
- grad_down_bias: float32 [768], P('tensor')
The draws below stay inside these ranges and needn't reach their ends.
All inputs are finite; a program needn't handle non-finite values.
Results may differ from the reference program's by a relative error of at most 0.012.
Values may be sent and summed in bfloat16 or wider, within the bound.
A program may use at most 128 MiB of HBM per device.

```python
import jax
import jax.numpy as jnp
from jax import lax

D = 768
HEADS = 12
HEAD_DIM = 64
FF = 3072
FRAMES = 1500
CLIPS = 8


def level_of(own_key, extent, cuts, smallest, top_value):
    level, own = 1.0, jax.random.fold_in(own_key, 6)
    for axis_at, blocks in cuts:
        steps = jnp.exp(jax.random.uniform(jax.random.fold_in(own, axis_at), (blocks,), jnp.float32, smallest / len(cuts), top_value / len(cuts)))
        level = level * jnp.repeat(steps, extent[axis_at] // blocks).reshape([-1 if axis == axis_at else 1 for axis in range(len(extent))])
    return level


def gaussian(stream_key, shape, width, limit, split=(), kind=jnp.bfloat16):
    gain = level_of(stream_key, shape, split, -0.22, 0.18) if split else 1.0
    values = jax.random.normal(stream_key, shape, jnp.float32) * width * gain
    return jnp.minimum(jnp.maximum(values, -limit), limit).astype(kind)


def setup_inputs(seed: int = 0) -> dict:
    seeds = jax.random.split(jax.random.key(seed), 15)
    tokens = gaussian(seeds[0], (CLIPS, FRAMES, D), 1.0, 6.0, ((0, 8), (1, 4)))
    ln1_gain = jnp.clip(1.0 + 0.1 * jax.random.normal(seeds[1], (D,), jnp.float32), 0.5, 1.5).astype(jnp.bfloat16)
    ln1_bias = gaussian(seeds[2], (D,), 0.5, 3.0)
    w_qkv = gaussian(seeds[3], (3, D, D), D ** -0.5, 0.21875, ((2, 4),))
    b_query_value = gaussian(seeds[4], (2, D), 0.5, 3.0, ((1, 4),))
    w_out = gaussian(seeds[5], (D, D), 2 ** -0.5, 4.0, ((0, 4),))
    b_out = gaussian(seeds[6], (D,), 0.5, 3.0)
    ln2_gain = jnp.clip(1.0 + 0.1 * jax.random.normal(seeds[7], (D,), jnp.float32), 0.5, 1.5).astype(jnp.bfloat16)
    ln2_bias = gaussian(seeds[8], (D,), 0.5, 3.0)
    w_up = gaussian(seeds[9], (D, FF), D ** -0.5, 0.21875, ((1, 4),))
    b_up = gaussian(seeds[10], (FF,), 0.5, 3.0, ((0, 4),))
    w_down = gaussian(seeds[11], (FF, D), FF ** -0.5, 0.109375, ((0, 4),))
    b_down = gaussian(seeds[12], (D,), 0.5, 3.0)
    cotangent = gaussian(seeds[13], (CLIPS, FRAMES, D), 1.0, 6.0, ((0, 8), (1, 4)))
    return {"tokens": tokens, "ln1_gain": ln1_gain, "ln1_bias": ln1_bias, "w_qkv": w_qkv, "b_query_value": b_query_value, "w_out": w_out, "b_out": b_out, "ln2_gain": ln2_gain, "ln2_bias": ln2_bias, "w_up": w_up, "b_up": b_up, "w_down": w_down, "b_down": b_down, "cotangent": cotangent}


@jax.custom_vjp
def low(v):
    return lax.optimization_barrier(v.astype(jnp.bfloat16)).astype(jnp.float32)

@jax.custom_vjp
def low_back(v):
    return v

def low_keep(v):
    return (low(v), None)

def low_pass(kept, grad):
    return (grad,)

def back_keep(v):
    return (v, None)

def back_low(kept, grad):
    return (low(grad),)
low.defvjp(low_keep, low_pass)
low_back.defvjp(back_keep, back_low)
norm_eps = 1e-05
highest = lax.Precision.HIGHEST

def layer_norm(values, gain_vec, shift_vec):
    center = values - lax.optimization_barrier(jnp.mean(values, axis=-1, keepdims=True))
    spread = lax.optimization_barrier(jnp.mean(center * center, axis=-1, keepdims=True))
    return center * lax.rsqrt(spread + norm_eps) * gain_vec + shift_vec

def attend_clip(triple):
    query_rows, key_rows, value_rows = triple
    scores = jnp.einsum('qhd,khd->hqk', query_rows, key_rows, precision=highest) * HEAD_DIM ** (-0.5)
    scores = low_back(scores)
    row_top = lax.optimization_barrier(jnp.max(scores, axis=-1, keepdims=True))
    expo_vals = jnp.exp(scores - row_top)
    probs = expo_vals / lax.optimization_barrier(jnp.sum(expo_vals, axis=-1, keepdims=True))
    return jnp.einsum('hqk,khd->qhd', low(probs), value_rows, precision=highest)

def forward(resid, gain_one, shift_one, w_qkv, b_qv, w_out, b_out, gain_two, shift_two, w_up, b_up, w_down, b_down):
    norm_one = low(layer_norm(resid, gain_one, shift_one))
    projected = jnp.einsum('cfd,jde->cfje', norm_one, w_qkv, precision=highest)
    bias_three = jnp.stack([b_qv[0], jnp.zeros_like(b_qv[0]), b_qv[1]])
    projected = low(low_back(projected + bias_three))
    split_heads = projected.reshape(CLIPS, FRAMES, 3, HEADS, HEAD_DIM)
    attended = lax.map(jax.checkpoint(attend_clip), (split_heads[:, :, 0], split_heads[:, :, 1], split_heads[:, :, 2]))
    attended = low(low_back(attended.reshape(CLIPS, FRAMES, D)))
    branch_one = low_back(jnp.einsum('cfe,ed->cfd', attended, w_out, precision=highest))
    hidden = resid + branch_one + b_out
    norm_two = low(layer_norm(hidden, gain_two, shift_two))
    pre_act = low_back(jnp.einsum('cfd,de->cfe', norm_two, w_up, precision=highest) + b_up)
    active = low(jax.nn.gelu(pre_act, approximate=False))
    branch_two = low_back(jnp.einsum('cfe,ed->cfd', active, w_down, precision=highest))
    return hidden + branch_two + b_down

def reference(tokens, ln1_gain, ln1_bias, w_qkv, b_query_value, w_out, b_out, ln2_gain, ln2_bias, w_up, b_up, w_down, b_down, cotangent):
    inputs = [arr.astype(jnp.float32) for arr in (tokens, ln1_gain, ln1_bias, w_qkv, b_query_value, w_out, b_out, ln2_gain, ln2_bias, w_up, b_up, w_down, b_down)]
    result, pullback = jax.vjp(forward, *inputs)
    grads = pullback(cotangent.astype(jnp.float32))
    return (result.astype(jnp.bfloat16), grads[0].astype(jnp.bfloat16), grads[1], grads[2], grads[3], grads[4], grads[5], grads[6], grads[7], grads[8], grads[9], grads[10], grads[11], grads[12])
```

```python
import functools

import jax
import jax.numpy as jnp
from jax import lax
from jax.experimental import pallas as pl
from jax.experimental.pallas import tpu as pltpu
from jax.sharding import PartitionSpec as P

HEAD_DIM = 64
norm_eps = 1e-05
MESH = pl.DeviceIdType.MESH
PIECES = 4
VMEM_BYTES = 56 * 1024 * 1024
F32 = jnp.float32
BF16 = jnp.bfloat16


def greet(axis, peers):
    barrier = pltpu.get_barrier_semaphore()
    for peer in peers:
        pl.semaphore_signal(barrier, inc=1, device_id={axis: peer}, device_id_type=MESH)
    pl.semaphore_wait(barrier, len(peers))


def remote(axis, src, dst, send, recv, peer):
    copy = pltpu.make_async_remote_copy(
        src_ref=src,
        dst_ref=dst,
        send_sem=send,
        recv_sem=recv,
        device_id={axis: peer},
        device_id_type=MESH,
    )
    copy.start()
    return copy


def tensor_peers():
    me = lax.axis_index("tensor")
    near = me + 1 - 2 * lax.rem(me, 2)
    far = lax.rem(me + 2, 4)
    corner = lax.rem(near + 2, 4)
    return me, near, far, corner


def gather_kernel(x_ref, o_ref, own_sem, far_send, far_recv, near_send, near_recv, pass_send, pass_recv):
    me, near, far, _ = tensor_peers()
    step = x_ref.shape[0] // PIECES
    greet("tensor", (near, far))
    far_copies = []
    for piece in range(PIECES):
        span = pl.ds(piece * step, step)
        far_copies.append(
            remote("tensor", x_ref.at[span], o_ref.at[me, span], far_send.at[piece], far_recv.at[piece], far)
        )
    near_copy = remote("tensor", x_ref, o_ref.at[me], near_send, near_recv, near)
    own = pltpu.make_async_copy(x_ref, o_ref.at[me], own_sem)
    own.start()
    passed = []
    for piece in range(PIECES):
        span = pl.ds(piece * step, step)
        far_copies[piece].wait_recv()
        passed.append(
            remote(
                "tensor", o_ref.at[far, span], o_ref.at[far, span], pass_send.at[piece], pass_recv.at[piece], near
            )
        )
    own.wait()
    near_copy.wait()
    for piece in range(PIECES):
        far_copies[piece].wait_send()
        passed[piece].wait()


def gather_rows(block):
    return pl.pallas_call(
        gather_kernel,
        out_shape=jax.ShapeDtypeStruct((4,) + block.shape, block.dtype),
        in_specs=[pl.BlockSpec(memory_space=pl.ANY)],
        out_specs=pl.BlockSpec(memory_space=pl.ANY),
        scratch_shapes=[
            pltpu.SemaphoreType.DMA,
            pltpu.SemaphoreType.DMA((PIECES,)),
            pltpu.SemaphoreType.DMA((PIECES,)),
            pltpu.SemaphoreType.DMA,
            pltpu.SemaphoreType.DMA,
            pltpu.SemaphoreType.DMA((PIECES,)),
            pltpu.SemaphoreType.DMA((PIECES,)),
        ],
        compiler_params=pltpu.CompilerParams(
            collective_id=0, has_side_effects=True, vmem_limit_bytes=VMEM_BYTES
        ),
        name="gather_rows",
    )(block)


def scatter_kernel(
    x_ref, o_ref, got_far, got_own, mixed, got_sum, a_send, a_recv, b_send, b_recv, c_send, c_recv
):
    me, near, far, corner = tensor_peers()
    step = x_ref.shape[1] // PIECES
    greet("tensor", (near, far))
    spans = [pl.ds(piece * step, step) for piece in range(PIECES)]
    first = [
        remote("tensor", x_ref.at[corner, span], got_far.at[span], a_send.at[i], a_recv.at[i], near)
        for i, span in enumerate(spans)
    ]
    second = remote("tensor", x_ref.at[near], got_own, b_send, b_recv, near)
    third = []
    for i, span in enumerate(spans):
        first[i].wait_recv()
        mixed[span] = (x_ref[far, span].astype(F32) + got_far[span].astype(F32)).astype(BF16)
        third.append(remote("tensor", mixed.at[span], got_sum.at[span], c_send.at[i], c_recv.at[i], far))
    second.wait_recv()
    for i, span in enumerate(spans):
        third[i].wait_recv()
        o_ref[span] = x_ref[me, span].astype(F32) + got_own[span].astype(F32) + got_sum[span].astype(F32)
    second.wait_send()
    for i in range(PIECES):
        first[i].wait_send()
        third[i].wait_send()


def scatter_sum(blocks):
    shape = blocks.shape[1:]
    return pl.pallas_call(
        scatter_kernel,
        out_shape=jax.ShapeDtypeStruct(shape, F32),
        in_specs=[pl.BlockSpec(memory_space=pltpu.VMEM)],
        out_specs=pl.BlockSpec(memory_space=pltpu.VMEM),
        scratch_shapes=[pltpu.VMEM(shape, BF16)] * 4
        + [
            pltpu.SemaphoreType.DMA((PIECES,)),
            pltpu.SemaphoreType.DMA((PIECES,)),
            pltpu.SemaphoreType.DMA,
            pltpu.SemaphoreType.DMA,
            pltpu.SemaphoreType.DMA((PIECES,)),
            pltpu.SemaphoreType.DMA((PIECES,)),
        ],
        compiler_params=pltpu.CompilerParams(
            collective_id=1, has_side_effects=True, vmem_limit_bytes=VMEM_BYTES
        ),
        name="scatter_sum",
    )(blocks)


def swap_kernel(x_ref, o_ref, own_sem, send, recv):
    me = lax.axis_index("seq")
    peers = [lax.rem(me + hop, 4) for hop in (2, 1, 3)]
    greet("seq", peers)
    copies = [
        remote("seq", x_ref.at[peer], o_ref.at[me], send.at[i], recv.at[i], peer)
        for i, peer in enumerate(peers)
    ]
    own = pltpu.make_async_copy(x_ref.at[me], o_ref.at[me], own_sem)
    own.start()
    own.wait()
    for copy in copies:
        copy.wait()


def swap_seq(blocks, ident):
    return pl.pallas_call(
        swap_kernel,
        out_shape=jax.ShapeDtypeStruct(blocks.shape, blocks.dtype),
        in_specs=[pl.BlockSpec(memory_space=pl.ANY)],
        out_specs=pl.BlockSpec(memory_space=pl.ANY),
        scratch_shapes=[
            pltpu.SemaphoreType.DMA,
            pltpu.SemaphoreType.DMA((3,)),
            pltpu.SemaphoreType.DMA((3,)),
        ],
        compiler_params=pltpu.CompilerParams(
            collective_id=ident, has_side_effects=True, vmem_limit_bytes=VMEM_BYTES
        ),
        name="swap_seq",
    )(blocks)


def rows_dot(a, b):
    return lax.dot_general(a, b, (((0,), (0,)), ((), ())), preferred_element_type=F32)


def cols_dot(a, b):
    return lax.dot_general(a, b, (((1,), (1,)), ((), ())), preferred_element_type=F32)


def side_by_side(ref):
    return jnp.concatenate([ref[i, 0] for i in range(ref.shape[0])], axis=1)


def masked_scores(key_cols, query_cols, span, real):
    scores = rows_dot(key_cols, query_cols)
    row = lax.broadcasted_iota(jnp.int32, (scores.shape[0], 1), 0)
    return jnp.where(lax.rem(row, span) < real, scores, -1e30)


def attend_kernel(real, q_ref, k_ref, v_ref, o_ref, lse_ref):
    shards, _, _, span = q_ref.shape
    key_cols, value_cols = side_by_side(k_ref), side_by_side(v_ref)
    for i in range(shards):
        scores = masked_scores(key_cols, q_ref[i, 0], span, real)
        top = jnp.max(scores, axis=0, keepdims=True)
        expo = jnp.exp(scores - top)
        total = jnp.sum(expo, axis=0, keepdims=True)
        probs = (expo * (1.0 / total)).astype(BF16)
        o_ref[i, 0] = jnp.dot(value_cols, probs, preferred_element_type=F32).astype(BF16)
        lse_ref[i, 0] = top + jnp.log(total)


def head_spec(shards, span, offset):
    return pl.BlockSpec((shards, 1, HEAD_DIM, span), lambda h: (0, offset + h, 0, 0))


def attend_forward(qkv, heads, real):
    shards, _, _, span = qkv.shape
    return pl.pallas_call(
        functools.partial(attend_kernel, real),
        grid=(heads,),
        out_shape=(
            jax.ShapeDtypeStruct((shards, heads, HEAD_DIM, span), BF16),
            jax.ShapeDtypeStruct((shards, heads, 1, span), F32),
        ),
        in_specs=[head_spec(shards, span, 0), head_spec(shards, span, heads), head_spec(shards, span, 2 * heads)],
        out_specs=(
            head_spec(shards, span, 0),
            pl.BlockSpec((shards, 1, 1, span), lambda h: (0, h, 0, 0)),
        ),
        compiler_params=pltpu.CompilerParams(vmem_limit_bytes=VMEM_BYTES),
        name="attend_forward",
    )(qkv, qkv, qkv)


def attend_back_kernel(real, q_ref, k_ref, v_ref, g_ref, lse_ref, dq_ref, dk_ref, dv_ref):
    shards, _, _, span = q_ref.shape
    key_cols, value_cols = side_by_side(k_ref), side_by_side(v_ref)
    grad_key, grad_value = None, None
    for i in range(shards):
        query, grad = q_ref[i, 0], g_ref[i, 0]
        scores = masked_scores(key_cols, query, span, real)
        probs = jnp.exp(scores - lse_ref[i, 0])
        grad_probs = rows_dot(value_cols, grad)
        inner = jnp.sum(probs * grad_probs, axis=0, keepdims=True)
        grad_scores = (probs * (grad_probs - inner)).astype(BF16)
        dq_ref[i, 0] = (
            jnp.dot(key_cols, grad_scores, preferred_element_type=F32) * HEAD_DIM ** (-0.5)
        ).astype(BF16)
        key_part = cols_dot(query, grad_scores)
        value_part = cols_dot(grad, probs.astype(BF16))
        grad_key = key_part if grad_key is None else grad_key + key_part
        grad_value = value_part if grad_value is None else grad_value + value_part
    for i in range(shards):
        dk_ref[i, 0] = grad_key[:, i * span : (i + 1) * span].astype(BF16)
        dv_ref[i, 0] = grad_value[:, i * span : (i + 1) * span].astype(BF16)


def attend_backward(qkv, grad, lse, heads, real):
    shards, _, _, span = qkv.shape
    lse_spec = pl.BlockSpec((shards, 1, 1, span), lambda h: (0, h, 0, 0))
    shape = jax.ShapeDtypeStruct((shards, heads, HEAD_DIM, span), BF16)
    return pl.pallas_call(
        functools.partial(attend_back_kernel, real),
        grid=(heads,),
        out_shape=(shape, shape, shape),
        in_specs=[
            head_spec(shards, span, 0),
            head_spec(shards, span, heads),
            head_spec(shards, span, 2 * heads),
            head_spec(shards, span, 0),
            lse_spec,
        ],
        out_specs=(head_spec(shards, span, 0),) * 3,
        compiler_params=pltpu.CompilerParams(vmem_limit_bytes=VMEM_BYTES),
        name="attend_backward",
    )(qkv, qkv, qkv, grad, lse)


def project_kernel(rows_ref, w_ref, b_ref, o_ref):
    total = cols_dot(w_ref[...], rows_ref[0]) + b_ref[...]
    width = total.shape[0] // 3
    o_ref[0, :width] = (total[:width].astype(BF16).astype(F32) * HEAD_DIM ** (-0.5)).astype(BF16)
    o_ref[0, width:] = total[width:].astype(BF16)


def project(rows, w_flat, bias):
    clips, span, depth = rows.shape
    width = w_flat.shape[0]
    return pl.pallas_call(
        project_kernel,
        grid=(clips,),
        out_shape=jax.ShapeDtypeStruct((clips, width, span), BF16),
        in_specs=[
            pl.BlockSpec((1, span, depth), lambda c: (c, 0, 0)),
            pl.BlockSpec((width, depth), lambda c: (0, 0)),
            pl.BlockSpec((width, 1), lambda c: (0, 0)),
        ],
        out_specs=pl.BlockSpec((1, width, span), lambda c: (c, 0, 0)),
        compiler_params=pltpu.CompilerParams(vmem_limit_bytes=VMEM_BYTES),
        name="project",
    )(rows, w_flat, bias)


def layer_norm(values, gain_vec, shift_vec):
    center = values - jnp.mean(values, axis=-1, keepdims=True)
    spread = jnp.mean(center * center, axis=-1, keepdims=True)
    return center * lax.rsqrt(spread + norm_eps) * gain_vec + shift_vec


def gelu_exact(values):
    return jax.nn.gelu(values, approximate=False)


def dot(spec, a, b):
    return jnp.einsum(spec, a, b, preferred_element_type=F32)


def on_device(
    tokens,
    ln1_gain,
    ln1_bias,
    w_qkv,
    b_query_value,
    w_out,
    b_out,
    ln2_gain,
    ln2_bias,
    w_up,
    b_up,
    w_down,
    b_down,
    cotangent,
):
    width = w_qkv.shape[2]
    depth = w_qkv.shape[1]
    heads = width // HEAD_DIM
    real = tokens.shape[1]
    span = -(-real // 128) * 128
    pad = ((0, span - real), (0, 0))
    resid = jnp.pad(tokens[0], pad).astype(F32)
    cot = jnp.pad(cotangent[0], pad)
    gain_one, shift_one = ln1_gain.astype(F32), ln1_bias.astype(F32)
    gain_two, shift_two = ln2_gain.astype(F32), ln2_bias.astype(F32)
    norm_one = layer_norm(resid, gain_one, shift_one).astype(BF16)
    rows_one = gather_rows(norm_one)
    clips = rows_one.shape[0]
    w_flat = jnp.swapaxes(w_qkv, 1, 2).reshape(3 * width, depth)
    bias_qv = b_query_value.astype(F32)
    bias_three = jnp.concatenate([bias_qv[0], jnp.zeros_like(bias_qv[0]), bias_qv[1]])[:, None]
    projected = project(rows_one, w_flat, bias_three)
    qkv = swap_seq(projected, 2).reshape(clips, 3 * heads, HEAD_DIM, span)
    attended, lse = attend_forward(qkv, heads, real)
    attended = swap_seq(attended.reshape(clips, width, span), 3)
    branch_one = scatter_sum(dot("cef,ed->cfd", attended, w_out).astype(BF16))
    hidden = resid + branch_one + b_out.astype(F32)
    norm_two = layer_norm(hidden, gain_two, shift_two).astype(BF16)
    rows_two = gather_rows(norm_two)
    cot_rows = lax.all_gather(cot, "tensor", axis=0, tiled=False)
    pre_act = dot("cfd,de->cfe", rows_two, w_up) + b_up.astype(F32)
    active = gelu_exact(pre_act).astype(BF16)
    grad_active = dot("cfd,ed->cfe", cot_rows, w_down)
    _, gelu_pull = jax.vjp(gelu_exact, pre_act)
    grad_pre = gelu_pull(grad_active)[0].astype(BF16)
    grad_norm_two = dot("cfe,de->cfd", grad_pre, w_up).astype(BF16)
    branch_two = lax.psum_scatter(
        dot("cfe,ed->cfd", active, w_down).astype(BF16), "tensor", scatter_dimension=0, tiled=False
    ).astype(F32)
    output = (hidden + branch_two + b_down.astype(F32)).astype(BF16)
    grad_down = dot("cfe,cfd->ed", active, cot_rows)
    grad_up_bias = jnp.sum(grad_pre, axis=(0, 1), dtype=F32)
    grad_up = dot("cfd,cfe->de", rows_two, grad_pre)
    grad_up, grad_down, grad_norm_two = lax.optimization_barrier(
        (grad_up.astype(BF16), grad_down.astype(BF16), grad_norm_two)
    )
    grad_up, grad_down = lax.psum((grad_up, grad_down), ("dp", "seq"))
    grad_norm_two = scatter_sum(grad_norm_two)

    _, pull_two = jax.vjp(layer_norm, hidden, gain_two, shift_two)
    grad_hidden, grad_gain_two, grad_shift_two = pull_two(grad_norm_two)
    grad_hidden = grad_hidden + cot.astype(F32)
    hidden_low = grad_hidden.astype(BF16)
    grad_rows = gather_rows(hidden_low)
    grad_att = dot("cfd,ed->cef", grad_rows, w_out).astype(BF16)
    grad_out = dot("cef,cfd->ed", attended, grad_rows)
    grad_att = swap_seq(grad_att, 3).reshape(clips, heads, HEAD_DIM, span)
    grads = attend_backward(qkv, grad_att, lse, heads, real)
    grad_qkv_cols = jnp.concatenate([g.reshape(clips, width, span) for g in grads], axis=1)
    grad_qkv_cols = swap_seq(grad_qkv_cols, 2)
    grad_norm_one = scatter_sum(dot("ckf,kd->cfd", grad_qkv_cols, w_flat).astype(BF16))
    bias_sums = jnp.sum(grad_qkv_cols, axis=(0, 2), dtype=F32).reshape(3, width)
    grad_qkv = dot("cfd,ckf->dk", rows_one, grad_qkv_cols)
    grad_qkv, grad_out = grad_qkv.astype(BF16), grad_out.astype(BF16)
    grad_qkv, grad_out = lax.psum((grad_qkv, grad_out), ("seq", "dp"))
    grad_qkv = jnp.swapaxes(grad_qkv.reshape(depth, 3, width), 0, 1).astype(F32)

    _, pull_one = jax.vjp(layer_norm, resid, gain_one, shift_one)
    grad_resid, grad_gain_one, grad_shift_one = pull_one(grad_norm_one)
    grad_tokens = (grad_hidden + grad_resid).astype(BF16)
    vectors = jnp.stack(
        [
            grad_gain_one,
            grad_shift_one,
            jnp.sum(grad_hidden, axis=0),
            grad_gain_two,
            grad_shift_two,
            jnp.sum(cot.astype(F32), axis=0),
        ]
    )
    me = lax.axis_index("tensor")
    parts = lax.axis_size("tensor")
    local = jnp.concatenate([bias_sums[0], bias_sums[2], grad_up_bias])
    placed = jnp.where(jnp.arange(parts)[:, None] == me, local[None], 0.0)
    flat = lax.psum(jnp.concatenate([vectors.reshape(-1), placed.reshape(-1)]), ("dp", "seq", "tensor"))
    vectors = lax.dynamic_slice_in_dim(flat[: vectors.size].reshape(vectors.shape), me * width, width, 1)
    local = lax.dynamic_slice_in_dim(flat[vectors.shape[0] * depth :].reshape(parts, -1), me, 1, 0)[0]
    return (
        output[None, :real],
        grad_tokens[None, :real],
        vectors[0],
        vectors[1],
        grad_qkv,
        local[: 2 * width].reshape(2, width),
        grad_out.astype(F32),
        vectors[2],
        vectors[3],
        vectors[4],
        grad_up.astype(F32),
        local[2 * width :],
        grad_down.astype(F32),
        vectors[5],
    )


def solution(mesh):
    in_specs = (
        P(("dp", "tensor"), "seq", None),
        P(),
        P(),
        P(None, None, "tensor"),
        P(None, "tensor"),
        P("tensor", None),
        P(),
        P(),
        P(),
        P(None, "tensor"),
        P("tensor"),
        P("tensor", None),
        P(),
        P(("dp", "tensor"), "seq", None),
    )
    out_specs = (
        P(("dp", "tensor"), "seq", None),
        P(("dp", "tensor"), "seq", None),
        P("tensor"),
        P("tensor"),
        P(None, None, "tensor"),
        P(None, "tensor"),
        P("tensor", None),
        P("tensor"),
        P("tensor"),
        P("tensor"),
        P(None, "tensor"),
        P("tensor"),
        P("tensor", None),
        P("tensor"),
    )
    return jax.shard_map(
        on_device, mesh=mesh, in_specs=in_specs, out_specs=out_specs, check_vma=False
    )
```

```python
import functools

import jax
import jax.numpy as jnp
from jax import lax
from jax.experimental import pallas as pl
from jax.experimental.pallas import tpu as pltpu
from jax.sharding import PartitionSpec as P

HEAD_DIM = 64
norm_eps = 1e-05
MESH = pl.DeviceIdType.MESH
PIECES = 4
VMEM_BYTES = 56 * 1024 * 1024
F32 = jnp.float32
BF16 = jnp.bfloat16


def greet(axis, peers):
    barrier = pltpu.get_barrier_semaphore()
    for peer in peers:
        pl.semaphore_signal(barrier, inc=1, device_id={axis: peer}, device_id_type=MESH)
    pl.semaphore_wait(barrier, len(peers))


def remote(axis, src, dst, send, recv, peer):
    copy = pltpu.make_async_remote_copy(
        src_ref=src,
        dst_ref=dst,
        send_sem=send,
        recv_sem=recv,
        device_id={axis: peer},
        device_id_type=MESH,
    )
    copy.start()
    return copy


def tensor_peers():
    me = lax.axis_index("tensor")
    near = me + 1 - 2 * lax.rem(me, 2)
    far = lax.rem(me + 2, 4)
    corner = lax.rem(near + 2, 4)
    return me, near, far, corner


def gather_kernel(x_ref, o_ref, own_sem, far_send, far_recv, near_send, near_recv, pass_send, pass_recv):
    me, near, far, _ = tensor_peers()
    step = x_ref.shape[0] // PIECES
    greet("tensor", (near, far))
    far_copies = []
    for piece in range(PIECES):
        span = pl.ds(piece * step, step)
        far_copies.append(
            remote("tensor", x_ref.at[span], o_ref.at[me, span], far_send.at[piece], far_recv.at[piece], far)
        )
    near_copy = remote("tensor", x_ref, o_ref.at[me], near_send, near_recv, near)
    own = pltpu.make_async_copy(x_ref, o_ref.at[me], own_sem)
    own.start()
    passed = []
    for piece in range(PIECES):
        span = pl.ds(piece * step, step)
        far_copies[piece].wait_recv()
        passed.append(
            remote(
                "tensor", o_ref.at[far, span], o_ref.at[far, span], pass_send.at[piece], pass_recv.at[piece], near
            )
        )
    own.wait()
    near_copy.wait()
    for piece in range(PIECES):
        far_copies[piece].wait_send()
        passed[piece].wait()


def gather_rows(block):
    return pl.pallas_call(
        gather_kernel,
        out_shape=jax.ShapeDtypeStruct((4,) + block.shape, block.dtype),
        in_specs=[pl.BlockSpec(memory_space=pl.ANY)],
        out_specs=pl.BlockSpec(memory_space=pl.ANY),
        scratch_shapes=[
            pltpu.SemaphoreType.DMA,
            pltpu.SemaphoreType.DMA((PIECES,)),
            pltpu.SemaphoreType.DMA((PIECES,)),
            pltpu.SemaphoreType.DMA,
            pltpu.SemaphoreType.DMA,
            pltpu.SemaphoreType.DMA((PIECES,)),
            pltpu.SemaphoreType.DMA((PIECES,)),
        ],
        compiler_params=pltpu.CompilerParams(
            collective_id=0, has_side_effects=True, vmem_limit_bytes=VMEM_BYTES
        ),
        name="gather_rows",
    )(block)


def scatter_kernel(
    x_ref, o_ref, got_far, got_own, mixed, got_sum, a_send, a_recv, b_send, b_recv, c_send, c_recv
):
    me, near, far, corner = tensor_peers()
    step = x_ref.shape[1] // PIECES
    greet("tensor", (near, far))
    spans = [pl.ds(piece * step, step) for piece in range(PIECES)]
    first = [
        remote("tensor", x_ref.at[corner, span], got_far.at[span], a_send.at[i], a_recv.at[i], near)
        for i, span in enumerate(spans)
    ]
    second = remote("tensor", x_ref.at[near], got_own, b_send, b_recv, near)
    third = []
    for i, span in enumerate(spans):
        first[i].wait_recv()
        mixed[span] = (x_ref[far, span].astype(F32) + got_far[span].astype(F32)).astype(BF16)
        third.append(remote("tensor", mixed.at[span], got_sum.at[span], c_send.at[i], c_recv.at[i], far))
    second.wait_recv()
    for i, span in enumerate(spans):
        third[i].wait_recv()
        o_ref[span] = x_ref[me, span].astype(F32) + got_own[span].astype(F32) + got_sum[span].astype(F32)
    second.wait_send()
    for i in range(PIECES):
        first[i].wait_send()
        third[i].wait_send()


def scatter_sum(blocks):
    shape = blocks.shape[1:]
    return pl.pallas_call(
        scatter_kernel,
        out_shape=jax.ShapeDtypeStruct(shape, F32),
        in_specs=[pl.BlockSpec(memory_space=pltpu.VMEM)],
        out_specs=pl.BlockSpec(memory_space=pltpu.VMEM),
        scratch_shapes=[pltpu.VMEM(shape, BF16)] * 4
        + [
            pltpu.SemaphoreType.DMA((PIECES,)),
            pltpu.SemaphoreType.DMA((PIECES,)),
            pltpu.SemaphoreType.DMA,
            pltpu.SemaphoreType.DMA,
            pltpu.SemaphoreType.DMA((PIECES,)),
            pltpu.SemaphoreType.DMA((PIECES,)),
        ],
        compiler_params=pltpu.CompilerParams(
            collective_id=1, has_side_effects=True, vmem_limit_bytes=VMEM_BYTES
        ),
        name="scatter_sum",
    )(blocks)


def scatter_both_kernel(
    x_ref, g_ref, o_ref, part_ref, got_far, got_own, mixed, got_sum, got_part,
    a_send, a_recv, b_send, b_recv, c_send, c_recv, p_send, p_recv
):
    me, near, far, corner = tensor_peers()
    here = lax.axis_index("seq")
    ring = [lax.rem(here + hop, 4) for hop in (2, 1, 3)]
    step = x_ref.shape[1] // PIECES
    barrier = pltpu.get_barrier_semaphore()
    for peer in (near, far):
        pl.semaphore_signal(barrier, inc=1, device_id={"tensor": peer}, device_id_type=MESH)
    for peer in ring:
        pl.semaphore_signal(barrier, inc=1, device_id={"seq": peer}, device_id_type=MESH)
    pl.semaphore_wait(barrier, 5)
    spans = [pl.ds(piece * step, step) for piece in range(PIECES)]
    first = [
        remote("tensor", x_ref.at[corner, span], got_far.at[span], a_send.at[i], a_recv.at[i], near)
        for i, span in enumerate(spans)
    ]
    second = remote("tensor", x_ref.at[near], got_own, b_send, b_recv, near)
    across = [
        remote("seq", g_ref.at[peer], got_part.at[i], p_send.at[i], p_recv.at[i], peer)
        for i, peer in enumerate(ring)
    ]
    third = []
    for i, span in enumerate(spans):
        first[i].wait_recv()
        mixed[span] = (x_ref[far, span].astype(F32) + got_far[span].astype(F32)).astype(BF16)
        third.append(remote("tensor", mixed.at[span], got_sum.at[span], c_send.at[i], c_recv.at[i], far))
    second.wait_recv()
    for i, span in enumerate(spans):
        third[i].wait_recv()
        o_ref[span] = x_ref[me, span].astype(F32) + got_own[span].astype(F32) + got_sum[span].astype(F32)
    total = g_ref[here].astype(F32)
    for i in range(3):
        across[i].wait_recv()
        total = total + got_part[i].astype(F32)
    part_ref[...] = total.astype(BF16)
    second.wait_send()
    for i in range(PIECES):
        first[i].wait_send()
        third[i].wait_send()
    for copy in across:
        copy.wait_send()


def scatter_both(blocks, grads):
    shape = blocks.shape[1:]
    return pl.pallas_call(
        scatter_both_kernel,
        out_shape=(jax.ShapeDtypeStruct(shape, F32), jax.ShapeDtypeStruct(grads.shape[1:], BF16)),
        in_specs=[pl.BlockSpec(memory_space=pltpu.VMEM)] * 2,
        out_specs=(pl.BlockSpec(memory_space=pltpu.VMEM),) * 2,
        scratch_shapes=[pltpu.VMEM(shape, BF16)] * 4
        + [pltpu.VMEM((3,) + grads.shape[1:], BF16)]
        + [
            pltpu.SemaphoreType.DMA((PIECES,)),
            pltpu.SemaphoreType.DMA((PIECES,)),
            pltpu.SemaphoreType.DMA,
            pltpu.SemaphoreType.DMA,
            pltpu.SemaphoreType.DMA((PIECES,)),
            pltpu.SemaphoreType.DMA((PIECES,)),
            pltpu.SemaphoreType.DMA((3,)),
            pltpu.SemaphoreType.DMA((3,)),
        ],
        compiler_params=pltpu.CompilerParams(
            collective_id=4, has_side_effects=True, vmem_limit_bytes=VMEM_BYTES
        ),
        name="scatter_both",
    )(blocks, grads)


def finish_kernel(
    dp_size, part_ref, vec_ref, local_ref, o_ref, vec_out,
    full, got_dp, got_vec, vec_sum, seq_vec, dp_vec, dp_mix,
    d_send, d_recv, a_send, a_recv, s_send, s_recv, e_send, e_recv, g_send, g_recv
):
    tensor_at, here, group = lax.axis_index("tensor"), lax.axis_index("seq"), lax.axis_index("dp")
    columns = [lax.rem(tensor_at + hop, 4) for hop in (1, 2, 3)]
    ring = [lax.rem(here + hop, 4) for hop in (2, 1, 3)]
    others = [lax.rem(group + hop, dp_size) for hop in range(1, dp_size)]
    barrier = pltpu.get_barrier_semaphore()
    for axis, peers in (("tensor", columns), ("seq", ring), ("dp", others)):
        for peer in peers:
            pl.semaphore_signal(barrier, inc=1, device_id={axis: peer}, device_id_type=MESH)
    pl.semaphore_wait(barrier, 6 + len(others))
    parts = [
        remote("dp", part_ref, got_dp.at[group], d_send.at[i], d_recv.at[i], peer) for i, peer in enumerate(others)
    ]
    vectors = [
        remote("tensor", vec_ref.at[peer], got_vec.at[i], a_send.at[i], a_recv.at[i], peer)
        for i, peer in enumerate(columns)
    ]
    got_dp[group] = part_ref[...]
    total = vec_ref[tensor_at]
    for i in range(3):
        vectors[i].wait_recv()
        total = total + got_vec[i]
    vec_sum[0:8] = total
    vec_sum[8:16] = local_ref[...]
    seq_vec[here] = vec_sum[...]
    around = [
        remote("seq", vec_sum, seq_vec.at[here], s_send.at[i], s_recv.at[i], peer) for i, peer in enumerate(ring)
    ]
    for copy in parts:
        copy.wait_recv()
    total = got_dp[0].astype(F32)
    for i in range(1, dp_size):
        total = total + got_dp[i].astype(F32)
    full[here] = total.astype(BF16)
    spread = [
        remote("seq", full.at[here], full.at[here], g_send.at[i], g_recv.at[i], peer) for i, peer in enumerate(ring)
    ]
    for copy in around:
        copy.wait_recv()
    dp_mix[...] = seq_vec[0] + seq_vec[1] + seq_vec[2] + seq_vec[3]
    dp_vec[group] = dp_mix[...]
    last = [
        remote("dp", dp_mix, dp_vec.at[group], e_send.at[i], e_recv.at[i], peer) for i, peer in enumerate(others)
    ]
    for copy in last:
        copy.wait_recv()
    total = dp_vec[0]
    for i in range(1, dp_size):
        total = total + dp_vec[i]
    vec_out[...] = total
    for copy in spread:
        copy.wait_recv()
    for i in range(4):
        o_ref[i] = full[i].astype(F32)
    for copy in parts + vectors + around + spread + last:
        copy.wait_send()


def finish(part, vectors, local, dp_size):
    rows, depth = part.shape
    vec = local.shape
    wide = (2 * vec[0], vec[1])
    vmem = pl.BlockSpec(memory_space=pltpu.VMEM)
    pair = lambda n: [pltpu.SemaphoreType.DMA((n,)), pltpu.SemaphoreType.DMA((n,))]
    return pl.pallas_call(
        functools.partial(finish_kernel, dp_size),
        out_shape=(jax.ShapeDtypeStruct((4, rows, depth), F32), jax.ShapeDtypeStruct(wide, F32)),
        in_specs=[vmem] * 3,
        out_specs=(vmem, vmem),
        scratch_shapes=[
            pltpu.VMEM((4, rows, depth), BF16),
            pltpu.VMEM((dp_size, rows, depth), BF16),
            pltpu.VMEM((3,) + vec, F32),
            pltpu.VMEM(wide, F32),
            pltpu.VMEM((4,) + wide, F32),
            pltpu.VMEM((dp_size,) + wide, F32),
            pltpu.VMEM(wide, F32),
        ]
        + pair(dp_size - 1)
        + pair(3)
        + pair(3)
        + pair(dp_size - 1)
        + pair(3),
        compiler_params=pltpu.CompilerParams(
            collective_id=5, has_side_effects=True, vmem_limit_bytes=VMEM_BYTES
        ),
        name="finish",
    )(part, vectors, local)


def swap_kernel(x_ref, o_ref, own_sem, send, recv):
    me = lax.axis_index("seq")
    peers = [lax.rem(me + hop, 4) for hop in (2, 1, 3)]
    greet("seq", peers)
    copies = [
        remote("seq", x_ref.at[peer], o_ref.at[me], send.at[i], recv.at[i], peer)
        for i, peer in enumerate(peers)
    ]
    own = pltpu.make_async_copy(x_ref.at[me], o_ref.at[me], own_sem)
    own.start()
    own.wait()
    for copy in copies:
        copy.wait()


def swap_seq(blocks, ident):
    return pl.pallas_call(
        swap_kernel,
        out_shape=jax.ShapeDtypeStruct(blocks.shape, blocks.dtype),
        in_specs=[pl.BlockSpec(memory_space=pl.ANY)],
        out_specs=pl.BlockSpec(memory_space=pl.ANY),
        scratch_shapes=[
            pltpu.SemaphoreType.DMA,
            pltpu.SemaphoreType.DMA((3,)),
            pltpu.SemaphoreType.DMA((3,)),
        ],
        compiler_params=pltpu.CompilerParams(
            collective_id=ident, has_side_effects=True, vmem_limit_bytes=VMEM_BYTES
        ),
        name="swap_seq",
    )(blocks)


def rows_dot(a, b):
    return lax.dot_general(a, b, (((0,), (0,)), ((), ())), preferred_element_type=F32)


def cols_dot(a, b):
    return lax.dot_general(a, b, (((1,), (1,)), ((), ())), preferred_element_type=F32)


def side_by_side(ref):
    return jnp.concatenate([ref[i, 0] for i in range(ref.shape[0])], axis=1)


def masked_scores(key_cols, query_cols, span, real):
    scores = rows_dot(key_cols, query_cols)
    row = lax.broadcasted_iota(jnp.int32, (scores.shape[0], 1), 0)
    return jnp.where(lax.rem(row, span) < real, scores, -1e30)


def attend_kernel(real, q_ref, k_ref, v_ref, o_ref, lse_ref):
    shards, _, _, span = q_ref.shape
    key_cols, value_cols = side_by_side(k_ref), side_by_side(v_ref)
    for i in range(shards):
        scores = masked_scores(key_cols, q_ref[i, 0], span, real)
        top = jnp.max(scores, axis=0, keepdims=True)
        expo = jnp.exp(scores - top)
        total = jnp.sum(expo, axis=0, keepdims=True)
        probs = (expo * (1.0 / total)).astype(BF16)
        o_ref[i, 0] = jnp.dot(value_cols, probs, preferred_element_type=F32).astype(BF16)
        lse_ref[i, 0] = top + jnp.log(total)


def head_spec(shards, span, offset):
    return pl.BlockSpec((shards, 1, HEAD_DIM, span), lambda h: (0, offset + h, 0, 0))


def attend_forward(qkv, heads, real):
    shards, _, _, span = qkv.shape
    return pl.pallas_call(
        functools.partial(attend_kernel, real),
        grid=(heads,),
        out_shape=(
            jax.ShapeDtypeStruct((shards, heads, HEAD_DIM, span), BF16),
            jax.ShapeDtypeStruct((shards, heads, 1, span), F32),
        ),
        in_specs=[head_spec(shards, span, 0), head_spec(shards, span, heads), head_spec(shards, span, 2 * heads)],
        out_specs=(
            head_spec(shards, span, 0),
            pl.BlockSpec((shards, 1, 1, span), lambda h: (0, h, 0, 0)),
        ),
        compiler_params=pltpu.CompilerParams(vmem_limit_bytes=VMEM_BYTES),
        name="attend_forward",
    )(qkv, qkv, qkv)


def attend_back_kernel(real, q_ref, k_ref, v_ref, g_ref, lse_ref, dq_ref, dk_ref, dv_ref):
    shards, _, _, span = q_ref.shape
    key_cols, value_cols = side_by_side(k_ref), side_by_side(v_ref)
    grad_key, grad_value = None, None
    for i in range(shards):
        query, grad = q_ref[i, 0], g_ref[i, 0]
        scores = masked_scores(key_cols, query, span, real)
        probs = jnp.exp(scores - lse_ref[i, 0])
        grad_probs = rows_dot(value_cols, grad)
        inner = jnp.sum(probs * grad_probs, axis=0, keepdims=True)
        grad_scores = (probs * (grad_probs - inner)).astype(BF16)
        dq_ref[i, 0] = (
            jnp.dot(key_cols, grad_scores, preferred_element_type=F32) * HEAD_DIM ** (-0.5)
        ).astype(BF16)
        key_part = cols_dot(query, grad_scores)
        value_part = cols_dot(grad, probs.astype(BF16))
        grad_key = key_part if grad_key is None else grad_key + key_part
        grad_value = value_part if grad_value is None else grad_value + value_part
    for i in range(shards):
        dk_ref[i, 0] = grad_key[:, i * span : (i + 1) * span].astype(BF16)
        dv_ref[i, 0] = grad_value[:, i * span : (i + 1) * span].astype(BF16)


def attend_backward(qkv, grad, lse, heads, real):
    shards, _, _, span = qkv.shape
    lse_spec = pl.BlockSpec((shards, 1, 1, span), lambda h: (0, h, 0, 0))
    shape = jax.ShapeDtypeStruct((shards, heads, HEAD_DIM, span), BF16)
    return pl.pallas_call(
        functools.partial(attend_back_kernel, real),
        grid=(heads,),
        out_shape=(shape, shape, shape),
        in_specs=[
            head_spec(shards, span, 0),
            head_spec(shards, span, heads),
            head_spec(shards, span, 2 * heads),
            head_spec(shards, span, 0),
            lse_spec,
        ],
        out_specs=(head_spec(shards, span, 0),) * 3,
        compiler_params=pltpu.CompilerParams(vmem_limit_bytes=VMEM_BYTES),
        name="attend_backward",
    )(qkv, qkv, qkv, grad, lse)


def project_kernel(rows_ref, w_ref, b_ref, o_ref):
    total = cols_dot(w_ref[...], rows_ref[0]) + b_ref[...]
    width = total.shape[0] // 3
    o_ref[0, :width] = (total[:width].astype(BF16).astype(F32) * HEAD_DIM ** (-0.5)).astype(BF16)
    o_ref[0, width:] = total[width:].astype(BF16)


def project(rows, w_flat, bias):
    clips, span, depth = rows.shape
    width = w_flat.shape[0]
    return pl.pallas_call(
        project_kernel,
        grid=(clips,),
        out_shape=jax.ShapeDtypeStruct((clips, width, span), BF16),
        in_specs=[
            pl.BlockSpec((1, span, depth), lambda c: (c, 0, 0)),
            pl.BlockSpec((width, depth), lambda c: (0, 0)),
            pl.BlockSpec((width, 1), lambda c: (0, 0)),
        ],
        out_specs=pl.BlockSpec((1, width, span), lambda c: (c, 0, 0)),
        compiler_params=pltpu.CompilerParams(vmem_limit_bytes=VMEM_BYTES),
        name="project",
    )(rows, w_flat, bias)


def layer_norm(values, gain_vec, shift_vec):
    center = values - jnp.mean(values, axis=-1, keepdims=True)
    spread = jnp.mean(center * center, axis=-1, keepdims=True)
    return center * lax.rsqrt(spread + norm_eps) * gain_vec + shift_vec


def gelu_exact(values):
    return jax.nn.gelu(values, approximate=False)


def dot(spec, a, b):
    return jnp.einsum(spec, a, b, preferred_element_type=F32)


def on_device(
    tokens,
    ln1_gain,
    ln1_bias,
    w_qkv,
    b_query_value,
    w_out,
    b_out,
    ln2_gain,
    ln2_bias,
    w_up,
    b_up,
    w_down,
    b_down,
    cotangent,
):
    width = w_qkv.shape[2]
    depth = w_qkv.shape[1]
    heads = width // HEAD_DIM
    real = tokens.shape[1]
    span = -(-real // 128) * 128
    pad = ((0, span - real), (0, 0))
    resid = jnp.pad(tokens[0], pad).astype(F32)
    cot = jnp.pad(cotangent[0], pad)
    gain_one, shift_one = ln1_gain.astype(F32), ln1_bias.astype(F32)
    gain_two, shift_two = ln2_gain.astype(F32), ln2_bias.astype(F32)
    norm_one = layer_norm(resid, gain_one, shift_one).astype(BF16)
    rows_one = gather_rows(norm_one)
    clips = rows_one.shape[0]
    w_flat = jnp.swapaxes(w_qkv, 1, 2).reshape(3 * width, depth)
    bias_qv = b_query_value.astype(F32)
    bias_three = jnp.concatenate([bias_qv[0], jnp.zeros_like(bias_qv[0]), bias_qv[1]])[:, None]
    projected = project(rows_one, w_flat, bias_three)
    qkv = swap_seq(projected, 2).reshape(clips, 3 * heads, HEAD_DIM, span)
    attended, lse = attend_forward(qkv, heads, real)
    attended = swap_seq(attended.reshape(clips, width, span), 3)
    branch_one = scatter_sum(dot("cef,ed->cfd", attended, w_out).astype(BF16))
    hidden = resid + branch_one + b_out.astype(F32)
    norm_two = layer_norm(hidden, gain_two, shift_two).astype(BF16)
    rows_two = gather_rows(norm_two)
    cot_rows = lax.all_gather(cot, "tensor", axis=0, tiled=False)
    pre_act = dot("cfd,de->cfe", rows_two, w_up) + b_up.astype(F32)
    active = gelu_exact(pre_act).astype(BF16)
    grad_active = dot("cfd,ed->cfe", cot_rows, w_down)
    _, gelu_pull = jax.vjp(gelu_exact, pre_act)
    grad_pre = gelu_pull(grad_active)[0].astype(BF16)
    grad_norm_two = dot("cfe,de->cfd", grad_pre, w_up).astype(BF16)
    branch_two = lax.psum_scatter(
        dot("cfe,ed->cfd", active, w_down).astype(BF16), "tensor", scatter_dimension=0, tiled=False
    )
    grad_down = dot("cfe,cfd->ed", active, cot_rows)
    grad_up_bias = jnp.sum(grad_pre, axis=(0, 1), dtype=F32)
    grad_up = dot("cfd,cfe->de", rows_two, grad_pre)
    grad_up, grad_down, grad_norm_two = lax.optimization_barrier(
        (grad_up.astype(BF16), grad_down.astype(BF16), grad_norm_two)
    )
    grad_norm_two = scatter_sum(grad_norm_two)

    _, pull_two = jax.vjp(layer_norm, hidden, gain_two, shift_two)
    grad_hidden, grad_gain_two, grad_shift_two = pull_two(grad_norm_two)
    grad_hidden = grad_hidden + cot.astype(F32)
    hidden_low = grad_hidden.astype(BF16)
    grad_rows = gather_rows(hidden_low)
    grad_att = dot("cfd,ed->cef", grad_rows, w_out).astype(BF16)
    grad_out = dot("cef,cfd->ed", attended, grad_rows).astype(BF16)
    grad_up, grad_down, grad_out, grad_att = lax.optimization_barrier((grad_up, grad_down, grad_out, grad_att))
    grad_up, grad_down, grad_out = lax.psum((grad_up, grad_down, grad_out), ("dp", "seq"))
    grad_att = swap_seq(grad_att, 3).reshape(clips, heads, HEAD_DIM, span)
    grads = attend_backward(qkv, grad_att, lse, heads, real)
    grad_qkv_cols = jnp.concatenate([g.reshape(clips, width, span) for g in grads], axis=1)
    grad_qkv_cols = swap_seq(grad_qkv_cols, 2)
    grad_norm_one = dot("ckf,kd->cfd", grad_qkv_cols, w_flat).astype(BF16)
    bias_sums = jnp.sum(grad_qkv_cols, axis=(0, 2), dtype=F32).reshape(3, width)
    grad_qkv = dot("ckf,cfd->kd", grad_qkv_cols, rows_one).astype(BF16)
    grad_up, grad_down, grad_out, branch_two, grad_norm_one = lax.optimization_barrier(
        (grad_up, grad_down, grad_out, branch_two, grad_norm_one)
    )
    output = (hidden + branch_two.astype(F32) + b_down.astype(F32)).astype(BF16)
    seq_size = lax.axis_size("seq")
    grad_norm_one, grad_part = scatter_both(grad_norm_one, grad_qkv.reshape(seq_size, -1, depth))

    _, pull_one = jax.vjp(layer_norm, resid, gain_one, shift_one)
    grad_resid, grad_gain_one, grad_shift_one = pull_one(grad_norm_one)
    grad_tokens = (grad_hidden + grad_resid).astype(BF16)
    vectors = jnp.stack(
        [
            grad_gain_one,
            grad_shift_one,
            jnp.sum(grad_hidden, axis=0),
            grad_gain_two,
            grad_shift_two,
            jnp.sum(cot.astype(F32), axis=0),
        ]
    )
    parts = depth // width
    lanes = -(-width // 128) * 128
    vectors = jnp.swapaxes(vectors.reshape(6, parts, width), 0, 1)
    vectors = jnp.pad(vectors, ((0, 0), (0, 2), (0, lanes - width)))
    hidden_parts = grad_up_bias.reshape(-1, width)
    local = jnp.concatenate([bias_sums[0][None], bias_sums[2][None], hidden_parts])
    local = jnp.pad(local, ((0, 8 - local.shape[0]), (0, lanes - width)))
    grad_qkv, small = finish(grad_part, vectors, local, lax.axis_size("dp"))
    grad_qkv = jnp.swapaxes(grad_qkv.reshape(3, width, depth), 1, 2)
    small = small[:, :width]
    return (
        output[None, :real],
        grad_tokens[None, :real],
        small[0],
        small[1],
        grad_qkv,
        small[8:10],
        grad_out.astype(F32),
        small[2],
        small[3],
        small[4],
        grad_up.astype(F32),
        small[10 : 10 + hidden_parts.shape[0]].reshape(-1),
        grad_down.astype(F32),
        small[5],
    )


def solution(mesh):
    in_specs = (
        P(("dp", "tensor"), "seq", None),
        P(),
        P(),
        P(None, None, "tensor"),
        P(None, "tensor"),
        P("tensor", None),
        P(),
        P(),
        P(),
        P(None, "tensor"),
        P("tensor"),
        P("tensor", None),
        P(),
        P(("dp", "tensor"), "seq", None),
    )
    out_specs = (
        P(("dp", "tensor"), "seq", None),
        P(("dp", "tensor"), "seq", None),
        P("tensor"),
        P("tensor"),
        P(None, None, "tensor"),
        P(None, "tensor"),
        P("tensor", None),
        P("tensor"),
        P("tensor"),
        P("tensor"),
        P(None, "tensor"),
        P("tensor"),
        P("tensor", None),
        P("tensor"),
    )
    return jax.shard_map(
        on_device, mesh=mesh, in_specs=in_specs, out_specs=out_specs, check_vma=False
    )
```

```python
import functools

import jax
import jax.numpy as jnp
from jax import lax
from jax.experimental import pallas as pl
from jax.experimental.pallas import tpu as pltpu
from jax.sharding import PartitionSpec as P

HEAD_DIM = 64
norm_eps = 1e-05
MESH = pl.DeviceIdType.MESH
PIECES = 4
VMEM_BYTES = 56 * 1024 * 1024
F32 = jnp.float32
BF16 = jnp.bfloat16


def greet(axis, peers):
    barrier = pltpu.get_barrier_semaphore()
    for peer in peers:
        pl.semaphore_signal(barrier, inc=1, device_id={axis: peer}, device_id_type=MESH)
    pl.semaphore_wait(barrier, len(peers))


def remote(axis, src, dst, send, recv, peer):
    copy = pltpu.make_async_remote_copy(
        src_ref=src,
        dst_ref=dst,
        send_sem=send,
        recv_sem=recv,
        device_id={axis: peer},
        device_id_type=MESH,
    )
    copy.start()
    return copy


def tensor_peers():
    me = lax.axis_index("tensor")
    near = me + 1 - 2 * lax.rem(me, 2)
    far = lax.rem(me + 2, 4)
    corner = lax.rem(near + 2, 4)
    return me, near, far, corner


def gather_kernel(x_ref, o_ref, own_sem, far_send, far_recv, near_send, near_recv, pass_send, pass_recv):
    me, near, far, _ = tensor_peers()
    step = x_ref.shape[0] // PIECES
    greet("tensor", (near, far))
    far_copies = []
    for piece in range(PIECES):
        span = pl.ds(piece * step, step)
        far_copies.append(
            remote("tensor", x_ref.at[span], o_ref.at[me, span], far_send.at[piece], far_recv.at[piece], far)
        )
    near_copy = remote("tensor", x_ref, o_ref.at[me], near_send, near_recv, near)
    own = pltpu.make_async_copy(x_ref, o_ref.at[me], own_sem)
    own.start()
    passed = []
    for piece in range(PIECES):
        span = pl.ds(piece * step, step)
        far_copies[piece].wait_recv()
        passed.append(
            remote(
                "tensor", o_ref.at[far, span], o_ref.at[far, span], pass_send.at[piece], pass_recv.at[piece], near
            )
        )
    own.wait()
    near_copy.wait()
    for piece in range(PIECES):
        far_copies[piece].wait_send()
        passed[piece].wait()


def gather_rows(block):
    return pl.pallas_call(
        gather_kernel,
        out_shape=jax.ShapeDtypeStruct((4,) + block.shape, block.dtype),
        in_specs=[pl.BlockSpec(memory_space=pl.ANY)],
        out_specs=pl.BlockSpec(memory_space=pl.ANY),
        scratch_shapes=[
            pltpu.SemaphoreType.DMA,
            pltpu.SemaphoreType.DMA((PIECES,)),
            pltpu.SemaphoreType.DMA((PIECES,)),
            pltpu.SemaphoreType.DMA,
            pltpu.SemaphoreType.DMA,
            pltpu.SemaphoreType.DMA((PIECES,)),
            pltpu.SemaphoreType.DMA((PIECES,)),
        ],
        compiler_params=pltpu.CompilerParams(
            collective_id=0, has_side_effects=True, vmem_limit_bytes=VMEM_BYTES
        ),
        name="gather_rows",
    )(block)


def scatter_kernel(
    x_ref, o_ref, got_far, got_own, mixed, got_sum, a_send, a_recv, b_send, b_recv, c_send, c_recv
):
    me, near, far, corner = tensor_peers()
    step = x_ref.shape[1] // PIECES
    greet("tensor", (near, far))
    spans = [pl.ds(piece * step, step) for piece in range(PIECES)]
    first = [
        remote("tensor", x_ref.at[corner, span], got_far.at[span], a_send.at[i], a_recv.at[i], near)
        for i, span in enumerate(spans)
    ]
    second = remote("tensor", x_ref.at[near], got_own, b_send, b_recv, near)
    third = []
    for i, span in enumerate(spans):
        first[i].wait_recv()
        mixed[span] = (x_ref[far, span].astype(F32) + got_far[span].astype(F32)).astype(BF16)
        third.append(remote("tensor", mixed.at[span], got_sum.at[span], c_send.at[i], c_recv.at[i], far))
    second.wait_recv()
    for i, span in enumerate(spans):
        third[i].wait_recv()
        o_ref[span] = x_ref[me, span].astype(F32) + got_own[span].astype(F32) + got_sum[span].astype(F32)
    second.wait_send()
    for i in range(PIECES):
        first[i].wait_send()
        third[i].wait_send()


def scatter_sum(blocks):
    shape = blocks.shape[1:]
    return pl.pallas_call(
        scatter_kernel,
        out_shape=jax.ShapeDtypeStruct(shape, F32),
        in_specs=[pl.BlockSpec(memory_space=pltpu.VMEM)],
        out_specs=pl.BlockSpec(memory_space=pltpu.VMEM),
        scratch_shapes=[pltpu.VMEM(shape, BF16)] * 4
        + [
            pltpu.SemaphoreType.DMA((PIECES,)),
            pltpu.SemaphoreType.DMA((PIECES,)),
            pltpu.SemaphoreType.DMA,
            pltpu.SemaphoreType.DMA,
            pltpu.SemaphoreType.DMA((PIECES,)),
            pltpu.SemaphoreType.DMA((PIECES,)),
        ],
        compiler_params=pltpu.CompilerParams(
            collective_id=1, has_side_effects=True, vmem_limit_bytes=VMEM_BYTES
        ),
        name="scatter_sum",
    )(blocks)


def scatter_both_kernel(
    x_ref, g_ref, o_ref, part_ref, got_far, got_own, mixed, got_sum, got_part,
    a_send, a_recv, b_send, b_recv, c_send, c_recv, p_send, p_recv
):
    me, near, far, corner = tensor_peers()
    here = lax.axis_index("seq")
    ring = [lax.rem(here + hop, 4) for hop in (2, 1, 3)]
    step = x_ref.shape[1] // PIECES
    barrier = pltpu.get_barrier_semaphore()
    for peer in (near, far):
        pl.semaphore_signal(barrier, inc=1, device_id={"tensor": peer}, device_id_type=MESH)
    for peer in ring:
        pl.semaphore_signal(barrier, inc=1, device_id={"seq": peer}, device_id_type=MESH)
    pl.semaphore_wait(barrier, 5)
    spans = [pl.ds(piece * step, step) for piece in range(PIECES)]
    first = [
        remote("tensor", x_ref.at[corner, span], got_far.at[span], a_send.at[i], a_recv.at[i], near)
        for i, span in enumerate(spans)
    ]
    second = remote("tensor", x_ref.at[near], got_own, b_send, b_recv, near)
    across = [
        remote("seq", g_ref.at[peer], got_part.at[i], p_send.at[i], p_recv.at[i], peer)
        for i, peer in enumerate(ring)
    ]
    third = []
    for i, span in enumerate(spans):
        first[i].wait_recv()
        mixed[span] = (x_ref[far, span].astype(F32) + got_far[span].astype(F32)).astype(BF16)
        third.append(remote("tensor", mixed.at[span], got_sum.at[span], c_send.at[i], c_recv.at[i], far))
    second.wait_recv()
    for i, span in enumerate(spans):
        third[i].wait_recv()
        o_ref[span] = x_ref[me, span].astype(F32) + got_own[span].astype(F32) + got_sum[span].astype(F32)
    total = g_ref[here].astype(F32)
    for i in range(3):
        across[i].wait_recv()
        total = total + got_part[i].astype(F32)
    part_ref[...] = total.astype(BF16)
    second.wait_send()
    for i in range(PIECES):
        first[i].wait_send()
        third[i].wait_send()
    for copy in across:
        copy.wait_send()


def scatter_both(blocks, grads):
    shape = blocks.shape[1:]
    return pl.pallas_call(
        scatter_both_kernel,
        out_shape=(jax.ShapeDtypeStruct(shape, F32), jax.ShapeDtypeStruct(grads.shape[1:], BF16)),
        in_specs=[pl.BlockSpec(memory_space=pltpu.VMEM)] * 2,
        out_specs=(pl.BlockSpec(memory_space=pltpu.VMEM),) * 2,
        scratch_shapes=[pltpu.VMEM(shape, BF16)] * 4
        + [pltpu.VMEM((3,) + grads.shape[1:], BF16)]
        + [
            pltpu.SemaphoreType.DMA((PIECES,)),
            pltpu.SemaphoreType.DMA((PIECES,)),
            pltpu.SemaphoreType.DMA,
            pltpu.SemaphoreType.DMA,
            pltpu.SemaphoreType.DMA((PIECES,)),
            pltpu.SemaphoreType.DMA((PIECES,)),
            pltpu.SemaphoreType.DMA((3,)),
            pltpu.SemaphoreType.DMA((3,)),
        ],
        compiler_params=pltpu.CompilerParams(
            collective_id=4, has_side_effects=True, vmem_limit_bytes=VMEM_BYTES
        ),
        name="scatter_both",
    )(blocks, grads)


def finish_kernel(
    dp_size, part_ref, vec_ref, local_ref, o_ref, vec_out,
    full, got_dp, got_vec, vec_sum, seq_vec, dp_vec, dp_mix,
    d_send, d_recv, a_send, a_recv, s_send, s_recv, e_send, e_recv, g_send, g_recv
):
    tensor_at, here, group = lax.axis_index("tensor"), lax.axis_index("seq"), lax.axis_index("dp")
    columns = [lax.rem(tensor_at + hop, 4) for hop in (1, 2, 3)]
    ring = [lax.rem(here + hop, 4) for hop in (2, 1, 3)]
    others = [lax.rem(group + hop, dp_size) for hop in range(1, dp_size)]
    barrier = pltpu.get_barrier_semaphore()
    for axis, peers in (("tensor", columns), ("seq", ring), ("dp", others)):
        for peer in peers:
            pl.semaphore_signal(barrier, inc=1, device_id={axis: peer}, device_id_type=MESH)
    pl.semaphore_wait(barrier, 6 + len(others))
    parts = [
        remote("dp", part_ref, got_dp.at[group], d_send.at[i], d_recv.at[i], peer) for i, peer in enumerate(others)
    ]
    vectors = [
        remote("tensor", vec_ref.at[peer], got_vec.at[i], a_send.at[i], a_recv.at[i], peer)
        for i, peer in enumerate(columns)
    ]
    got_dp[group] = part_ref[...]
    total = vec_ref[tensor_at]
    for i in range(3):
        vectors[i].wait_recv()
        total = total + got_vec[i]
    vec_sum[0:8] = total
    vec_sum[8:16] = local_ref[...]
    seq_vec[here] = vec_sum[...]
    around = [
        remote("seq", vec_sum, seq_vec.at[here], s_send.at[i], s_recv.at[i], peer) for i, peer in enumerate(ring)
    ]
    for copy in parts:
        copy.wait_recv()
    total = got_dp[0].astype(F32)
    for i in range(1, dp_size):
        total = total + got_dp[i].astype(F32)
    full[here] = total.astype(BF16)
    spread = [
        remote("seq", full.at[here], full.at[here], g_send.at[i], g_recv.at[i], peer) for i, peer in enumerate(ring)
    ]
    for copy in around:
        copy.wait_recv()
    dp_mix[...] = seq_vec[0] + seq_vec[1] + seq_vec[2] + seq_vec[3]
    dp_vec[group] = dp_mix[...]
    last = [
        remote("dp", dp_mix, dp_vec.at[group], e_send.at[i], e_recv.at[i], peer) for i, peer in enumerate(others)
    ]
    for copy in last:
        copy.wait_recv()
    total = dp_vec[0]
    for i in range(1, dp_size):
        total = total + dp_vec[i]
    vec_out[...] = total
    for copy in spread:
        copy.wait_recv()
    for i in range(4):
        o_ref[i] = full[i].astype(F32)
    for copy in parts + vectors + around + spread + last:
        copy.wait_send()


def finish(part, vectors, local, dp_size):
    rows, depth = part.shape
    vec = local.shape
    wide = (2 * vec[0], vec[1])
    vmem = pl.BlockSpec(memory_space=pltpu.VMEM)
    pair = lambda n: [pltpu.SemaphoreType.DMA((n,)), pltpu.SemaphoreType.DMA((n,))]
    return pl.pallas_call(
        functools.partial(finish_kernel, dp_size),
        out_shape=(jax.ShapeDtypeStruct((4, rows, depth), F32), jax.ShapeDtypeStruct(wide, F32)),
        in_specs=[vmem] * 3,
        out_specs=(vmem, vmem),
        scratch_shapes=[
            pltpu.VMEM((4, rows, depth), BF16),
            pltpu.VMEM((dp_size, rows, depth), BF16),
            pltpu.VMEM((3,) + vec, F32),
            pltpu.VMEM(wide, F32),
            pltpu.VMEM((4,) + wide, F32),
            pltpu.VMEM((dp_size,) + wide, F32),
            pltpu.VMEM(wide, F32),
        ]
        + pair(dp_size - 1)
        + pair(3)
        + pair(3)
        + pair(dp_size - 1)
        + pair(3),
        compiler_params=pltpu.CompilerParams(
            collective_id=5, has_side_effects=True, vmem_limit_bytes=VMEM_BYTES
        ),
        name="finish",
    )(part, vectors, local)


def rows_dot(a, b):
    return lax.dot_general(a, b, (((0,), (0,)), ((), ())), preferred_element_type=F32)


def cols_dot(a, b):
    return lax.dot_general(a, b, (((1,), (1,)), ((), ())), preferred_element_type=F32)


def seq_ring(me):
    return [lax.rem(me + hop, 4) for hop in (2, 1, 3)]


def head_cols(ref, head, first):
    return jnp.concatenate([ref[i, head, first : first + HEAD_DIM] for i in range(ref.shape[0])], axis=1)


def masked_scores(key_cols, query_cols, span, real):
    scores = rows_dot(key_cols, query_cols)
    row = lax.broadcasted_iota(jnp.int32, (scores.shape[0], 1), 0)
    return jnp.where(lax.rem(row, span) < real, scores, -1e30)


def chunk(src, dst, send, recv, peer):
    return pltpu.make_async_remote_copy(
        src_ref=src, dst_ref=dst, send_sem=send, recv_sem=recv, device_id={"seq": peer}, device_id_type=MESH
    )


def attend_kernel(real, x_ref, qkv_ref, o_ref, lse_ref, got, att, back, x_send, x_recv, o_send, o_recv):
    me = lax.axis_index("seq")
    ring = seq_ring(me)
    _, heads, _, span = x_ref.shape
    greet("seq", ring)

    def arrival(h, k):
        return chunk(x_ref.at[ring[k], h], got.at[me, h], x_send.at[h, k], x_recv.at[h, k], ring[k])

    def result(h, k):
        return chunk(att.at[ring[k], h], back.at[me, h], o_send.at[h, k], o_recv.at[h, k], ring[k])

    for h in range(heads):
        for k in range(3):
            arrival(h, k).start()
    got[me] = x_ref[me]

    def one_head(h, carry):
        for k in range(3):
            arrival(h, k).wait_recv()
        key_cols, value_cols = head_cols(got, h, HEAD_DIM), head_cols(got, h, 2 * HEAD_DIM)
        for k, i in enumerate(ring + [me]):
            scores = masked_scores(key_cols, got[i, h, 0:HEAD_DIM], span, real)
            top = jnp.max(scores, axis=0, keepdims=True)
            expo = jnp.exp(scores - top)
            total = jnp.sum(expo, axis=0, keepdims=True)
            probs = (expo * (1.0 / total)).astype(BF16)
            out = jnp.dot(value_cols, probs, preferred_element_type=F32).astype(BF16)
            lse_ref[i, h] = top + jnp.log(total)
            if k < 3:
                att[i, h] = out
                result(h, k).start()
            else:
                back[me, h] = out
        return carry

    lax.fori_loop(0, heads, one_head, 0)
    qkv_ref[...] = got[...]
    for h in range(heads):
        for k in range(3):
            arrival(h, k).wait_send()
            result(h, k).wait()
    o_ref[...] = back[...]


def attend_forward(blocks, real):
    shards, heads, wide, span = blocks.shape
    vmem = pl.BlockSpec(memory_space=pltpu.VMEM)
    small = (shards, heads, HEAD_DIM, span)
    return pl.pallas_call(
        functools.partial(attend_kernel, real),
        out_shape=(
            jax.ShapeDtypeStruct(blocks.shape, BF16),
            jax.ShapeDtypeStruct(small, BF16),
            jax.ShapeDtypeStruct((shards, heads, 1, span), F32),
        ),
        in_specs=[vmem],
        out_specs=(vmem,) * 3,
        scratch_shapes=[pltpu.VMEM(blocks.shape, BF16), pltpu.VMEM(small, BF16), pltpu.VMEM(small, BF16)]
        + [pltpu.SemaphoreType.DMA((heads, 3))] * 4,
        compiler_params=pltpu.CompilerParams(
            collective_id=2, has_side_effects=True, vmem_limit_bytes=VMEM_BYTES
        ),
        name="attend_forward",
    )(blocks)


def attend_back_kernel(real, g_ref, qkv_ref, lse_ref, o_ref, got, work, back, x_send, x_recv, o_send, o_recv):
    me = lax.axis_index("seq")
    ring = seq_ring(me)
    shards, heads, _, span = g_ref.shape
    greet("seq", ring)

    def arrival(h, k):
        return chunk(g_ref.at[ring[k], h], got.at[me, h], x_send.at[h, k], x_recv.at[h, k], ring[k])

    def result(h, k):
        return chunk(work.at[ring[k], h], back.at[me, h], o_send.at[h, k], o_recv.at[h, k], ring[k])

    for h in range(heads):
        for k in range(3):
            arrival(h, k).start()
    got[me] = g_ref[me]

    def one_head(h, carry):
        for k in range(3):
            arrival(h, k).wait_recv()
        key_cols, value_cols = head_cols(qkv_ref, h, HEAD_DIM), head_cols(qkv_ref, h, 2 * HEAD_DIM)
        grad_key, grad_value = None, None
        for i in range(shards):
            query, grad = qkv_ref[i, h, 0:HEAD_DIM], got[i, h]
            scores = masked_scores(key_cols, query, span, real)
            probs = jnp.exp(scores - lse_ref[i, h])
            grad_probs = rows_dot(value_cols, grad)
            inner = jnp.sum(probs * grad_probs, axis=0, keepdims=True)
            grad_scores = (probs * (grad_probs - inner)).astype(BF16)
            work[i, h, 0:HEAD_DIM] = (
                jnp.dot(key_cols, grad_scores, preferred_element_type=F32) * HEAD_DIM ** (-0.5)
            ).astype(BF16)
            key_part = cols_dot(query, grad_scores)
            value_part = cols_dot(grad, probs.astype(BF16))
            grad_key = key_part if grad_key is None else grad_key + key_part
            grad_value = value_part if grad_value is None else grad_value + value_part
        for i in range(shards):
            piece = slice(i * span, (i + 1) * span)
            work[i, h, HEAD_DIM : 2 * HEAD_DIM] = grad_key[:, piece].astype(BF16)
            work[i, h, 2 * HEAD_DIM : 3 * HEAD_DIM] = grad_value[:, piece].astype(BF16)
        for k in range(3):
            result(h, k).start()
        back[me, h] = work[me, h]
        return carry

    lax.fori_loop(0, heads, one_head, 0)
    for h in range(heads):
        for k in range(3):
            arrival(h, k).wait_send()
            result(h, k).wait()
    o_ref[...] = back[...]


def attend_backward(grad, qkv, lse, real):
    heads = qkv.shape[1]
    vmem = pl.BlockSpec(memory_space=pltpu.VMEM)
    return pl.pallas_call(
        functools.partial(attend_back_kernel, real),
        out_shape=jax.ShapeDtypeStruct(qkv.shape, BF16),
        in_specs=[vmem] * 3,
        out_specs=vmem,
        scratch_shapes=[pltpu.VMEM(grad.shape, BF16), pltpu.VMEM(qkv.shape, BF16), pltpu.VMEM(qkv.shape, BF16)]
        + [pltpu.SemaphoreType.DMA((heads, 3))] * 4,
        compiler_params=pltpu.CompilerParams(
            collective_id=3, has_side_effects=True, vmem_limit_bytes=VMEM_BYTES
        ),
        name="attend_backward",
    )(grad, qkv, lse)


def project_kernel(rows_ref, w_ref, b_ref, s_ref, o_ref):
    total = cols_dot(w_ref[...], rows_ref[0]) + b_ref[...]
    o_ref[0] = (total.astype(BF16).astype(F32) * s_ref[...]).astype(BF16)


def project(rows, w_flat, bias, scale):
    clips, span, depth = rows.shape
    width = w_flat.shape[0]
    return pl.pallas_call(
        project_kernel,
        grid=(clips,),
        out_shape=jax.ShapeDtypeStruct((clips, width, span), BF16),
        in_specs=[
            pl.BlockSpec((1, span, depth), lambda c: (c, 0, 0)),
            pl.BlockSpec((width, depth), lambda c: (0, 0)),
            pl.BlockSpec((width, 1), lambda c: (0, 0)),
            pl.BlockSpec((width, 1), lambda c: (0, 0)),
        ],
        out_specs=pl.BlockSpec((1, width, span), lambda c: (c, 0, 0)),
        compiler_params=pltpu.CompilerParams(vmem_limit_bytes=VMEM_BYTES),
        name="project",
    )(rows, w_flat, bias, scale)


def layer_norm(values, gain_vec, shift_vec):
    center = values - jnp.mean(values, axis=-1, keepdims=True)
    spread = jnp.mean(center * center, axis=-1, keepdims=True)
    return center * lax.rsqrt(spread + norm_eps) * gain_vec + shift_vec


def gelu_exact(values):
    return jax.nn.gelu(values, approximate=False)


def dot(spec, a, b):
    return jnp.einsum(spec, a, b, preferred_element_type=F32)


def on_device(
    tokens,
    ln1_gain,
    ln1_bias,
    w_qkv,
    b_query_value,
    w_out,
    b_out,
    ln2_gain,
    ln2_bias,
    w_up,
    b_up,
    w_down,
    b_down,
    cotangent,
):
    width = w_qkv.shape[2]
    depth = w_qkv.shape[1]
    heads = width // HEAD_DIM
    real = tokens.shape[1]
    span = -(-real // 128) * 128
    pad = ((0, span - real), (0, 0))
    resid = jnp.pad(tokens[0], pad).astype(F32)
    cot = jnp.pad(cotangent[0], pad)
    gain_one, shift_one = ln1_gain.astype(F32), ln1_bias.astype(F32)
    gain_two, shift_two = ln2_gain.astype(F32), ln2_bias.astype(F32)
    norm_one = layer_norm(resid, gain_one, shift_one).astype(BF16)
    rows_one = gather_rows(norm_one)
    clips = rows_one.shape[0]
    w_flat = w_qkv.reshape(3, depth, heads, HEAD_DIM).transpose(2, 0, 3, 1).reshape(3 * width, depth)
    bias_qv = b_query_value.astype(F32)
    bias_three = jnp.stack([bias_qv[0], jnp.zeros_like(bias_qv[0]), bias_qv[1]])
    bias_three = bias_three.reshape(3, heads, HEAD_DIM).swapaxes(0, 1).reshape(-1, 1)
    row = jnp.arange(3 * width)[:, None]
    scale = jnp.where(row % (3 * HEAD_DIM) < HEAD_DIM, HEAD_DIM ** (-0.5), 1.0).astype(F32)
    projected = project(rows_one, w_flat, bias_three, scale)
    qkv, attended, lse = attend_forward(projected.reshape(clips, heads, 3 * HEAD_DIM, span), real)
    attended = attended.reshape(clips, width, span)
    branch_one = scatter_sum(dot("cef,ed->cfd", attended, w_out).astype(BF16))
    hidden = resid + branch_one + b_out.astype(F32)
    norm_two = layer_norm(hidden, gain_two, shift_two).astype(BF16)
    rows_two = gather_rows(norm_two)
    cot_rows = lax.all_gather(cot, "tensor", axis=0, tiled=False)
    pre_act = dot("cfd,de->cfe", rows_two, w_up) + b_up.astype(F32)
    active = gelu_exact(pre_act).astype(BF16)
    grad_active = dot("cfd,ed->cfe", cot_rows, w_down)
    _, gelu_pull = jax.vjp(gelu_exact, pre_act)
    grad_pre = gelu_pull(grad_active)[0].astype(BF16)
    grad_norm_two = dot("cfe,de->cfd", grad_pre, w_up).astype(BF16)
    branch_two = lax.psum_scatter(
        dot("cfe,ed->cfd", active, w_down).astype(BF16), "tensor", scatter_dimension=0, tiled=False
    )
    grad_down = dot("cfe,cfd->ed", active, cot_rows)
    grad_up_bias = jnp.sum(grad_pre, axis=(0, 1), dtype=F32)
    grad_up = dot("cfd,cfe->de", rows_two, grad_pre)
    grad_up, grad_down, grad_norm_two = lax.optimization_barrier(
        (grad_up.astype(BF16), grad_down.astype(BF16), grad_norm_two)
    )
    grad_up, grad_down = lax.psum((grad_up, grad_down), ("dp", "seq"))
    grad_norm_two = scatter_sum(grad_norm_two)

    _, pull_two = jax.vjp(layer_norm, hidden, gain_two, shift_two)
    grad_hidden, grad_gain_two, grad_shift_two = pull_two(grad_norm_two)
    grad_hidden = grad_hidden + cot.astype(F32)
    hidden_low = grad_hidden.astype(BF16)
    grad_rows = gather_rows(hidden_low)
    grad_att = dot("cfd,ed->cef", grad_rows, w_out).astype(BF16)
    grad_out = dot("cef,cfd->ed", attended, grad_rows).astype(BF16)
    grads = attend_backward(grad_att.reshape(clips, heads, HEAD_DIM, span), qkv, lse, real)
    grad_qkv_cols = grads.reshape(clips, 3 * width, span)
    grad_norm_one = dot("ckf,kd->cfd", grad_qkv_cols, w_flat).astype(BF16)
    bias_sums = jnp.sum(grad_qkv_cols, axis=(0, 2), dtype=F32).reshape(heads, 3, HEAD_DIM)
    grad_qkv = dot("ckf,cfd->kd", grad_qkv_cols, rows_one).astype(BF16)
    seq_size = lax.axis_size("seq")
    mine = jnp.concatenate([grad_qkv, grad_out]).reshape(seq_size, -1, depth)
    grad_norm_one, grad_part = scatter_both(grad_norm_one, mine)

    _, pull_one = jax.vjp(layer_norm, resid, gain_one, shift_one)
    grad_resid, grad_gain_one, grad_shift_one = pull_one(grad_norm_one)
    grad_tokens = (grad_hidden + grad_resid).astype(BF16)
    vectors = jnp.stack(
        [
            grad_gain_one,
            grad_shift_one,
            jnp.sum(grad_hidden, axis=0),
            grad_gain_two,
            grad_shift_two,
            jnp.sum(cot.astype(F32), axis=0),
        ]
    )
    parts = depth // width
    lanes = -(-width // 128) * 128
    vectors = jnp.swapaxes(vectors.reshape(6, parts, width), 0, 1)
    vectors = jnp.pad(vectors, ((0, 0), (0, 2), (0, lanes - width)))
    hidden_parts = grad_up_bias.reshape(-1, width)
    local = jnp.concatenate([bias_sums[:, 0].reshape(1, -1), bias_sums[:, 2].reshape(1, -1), hidden_parts])
    local = jnp.pad(local, ((0, 8 - local.shape[0]), (0, lanes - width)))
    grad_up, grad_down, branch_two, vectors = lax.optimization_barrier((grad_up, grad_down, branch_two, vectors))
    output = (hidden + branch_two.astype(F32) + b_down.astype(F32)).astype(BF16)
    mine, small = finish(grad_part, vectors, local, lax.axis_size("dp"))
    mine = mine.reshape(-1, depth)
    grad_qkv = mine[: 3 * width].reshape(heads, 3, HEAD_DIM, depth).transpose(1, 3, 0, 2).reshape(3, depth, width)
    small = small[:, :width]
    return (
        output[None, :real],
        grad_tokens[None, :real],
        small[0],
        small[1],
        grad_qkv,
        small[8:10],
        mine[3 * width :],
        small[2],
        small[3],
        small[4],
        grad_up.astype(F32),
        small[10 : 10 + hidden_parts.shape[0]].reshape(-1),
        grad_down.astype(F32),
        small[5],
    )


def solution(mesh):
    in_specs = (
        P(("dp", "tensor"), "seq", None),
        P(),
        P(),
        P(None, None, "tensor"),
        P(None, "tensor"),
        P("tensor", None),
        P(),
        P(),
        P(),
        P(None, "tensor"),
        P("tensor"),
        P("tensor", None),
        P(),
        P(("dp", "tensor"), "seq", None),
    )
    out_specs = (
        P(("dp", "tensor"), "seq", None),
        P(("dp", "tensor"), "seq", None),
        P("tensor"),
        P("tensor"),
        P(None, None, "tensor"),
        P(None, "tensor"),
        P("tensor", None),
        P("tensor"),
        P("tensor"),
        P("tensor"),
        P(None, "tensor"),
        P("tensor"),
        P("tensor", None),
        P("tensor"),
    )
    return jax.shard_map(
        on_device, mesh=mesh, in_specs=in_specs, out_specs=out_specs, check_vma=False
    )
```
